32 devices in a mesh: narrow: 4 (over x, core), wide: 8 (over z, y).
Axes of the slice: x: 2, y: 2, z: 4, core: 2. Of those that a mesh axis runs over, the one named last changes fastest.
Arguments:
- series: bfloat16 [4096, 1024], P('wide', 'narrow'), may hold values from -6 to 6
- reduction: bfloat16 [1024, 512], P('narrow'), may hold values from -0.1875 to 0.1875
- unmixing: float32 [512, 512], P('wide'), may hold values from -0.25 to 0.25
Outputs:
- sources: bfloat16 [4096, 512], P(('wide', 'narrow'))
- unmixed: float32 [512, 512], P('wide')
The draws below stay inside these ranges and needn't reach their ends.
All inputs are finite; a program needn't handle non-finite values.
Results may differ from the reference program's by a relative error of at most 0.0063.
Values may be sent and summed in bfloat16 or wider, within the bound.
No kernel may reach another device: no remote copies, remote signals or barrier semaphores. Data moves between devices by JAX's collectives and lax.ppermute only.
A program may use at most 64 MiB of HBM per device.

```python
import jax
import jax.numpy as jnp
from jax import lax

COMPS = 512
ITERS = 2
GRAY = 4096
TIMES = 1024


def level_of(stream_key, extent, split, low, high):
    gain = 1.0
    for position, shards_of in split:
        steps = jax.random.uniform(jax.random.fold_in(jax.random.fold_in(stream_key, 6), position), (shards_of,), jnp.float32, low / len(split), high / len(split))
        gain = gain * jnp.repeat(jnp.exp(steps), extent[position] // shards_of).reshape((-1,) + (1,) * (len(extent) - 1 - position))
    return gain


def scatter_about(key, shape, scale, bound, split=(), held_as=jnp.bfloat16):
    level = level_of(key, shape, split, -0.22, 0.18) if split else 1.0
    values = jax.random.normal(key, shape, jnp.float32) * scale * level
    return jnp.minimum(jnp.maximum(values, -bound), bound).astype(held_as)


def setup_inputs(seed: int = 0) -> dict:
    splits = jax.random.split(jax.random.key(seed), 4)
    series = scatter_about(splits[0], (GRAY, TIMES), 1.0, 6.0, ((0, 8), (1, 4)))
    reduction = scatter_about(splits[1], (TIMES, COMPS), TIMES ** -0.5, 0.1875, ((0, 4),))
    unmixing = scatter_about(splits[2], (COMPS, COMPS), COMPS ** -0.5, 0.25, ((0, 8),), jnp.float32)
    return {"series": series, "reduction": reduction, "unmixing": unmixing}


def transposed(left, right):
    return lax.dot_general(left, right, (((1,), (1,)), ((), ())), preferred_element_type=jnp.float32)

def reference(series, reduction, unmixing):
    reduced = jnp.dot(series, reduction, preferred_element_type=jnp.float32).astype(jnp.bfloat16)
    weights = unmixing
    eye_full = jnp.eye(COMPS, dtype=jnp.float32)
    for step in range(ITERS):
        activity = transposed(reduced, weights.astype(jnp.bfloat16))
        squashed = jnp.tanh(activity).astype(jnp.bfloat16)
        flat = activity.astype(jnp.bfloat16)
        moment = lax.dot_general(squashed, flat, (((0,), (0,)), ((), ())), preferred_element_type=jnp.float32)
        gradient = eye_full - moment / GRAY
        size_now = jnp.sqrt(jnp.sum(gradient * gradient))
        rate = 0.25 * jnp.sqrt(jnp.float32(COMPS)) / jnp.maximum(size_now, 1.0)
        weights = weights + rate * jnp.dot(gradient, weights, precision=lax.Precision.HIGHEST)
    sources = transposed(reduced, weights.astype(jnp.bfloat16)).astype(jnp.bfloat16)
    return (sources, weights)
```

```python
import functools

import jax
import jax.numpy as jnp
from jax import lax
from jax.experimental import pallas as pl
from jax.experimental.pallas import tpu as pltpu
from jax.sharding import PartitionSpec as P

ITERS = 2
CHUNK_BYTES = 4 * 1024 * 1024
AXES = ("narrow", "wide")
VMEM = pl.BlockSpec(memory_space=pltpu.VMEM)
SMEM = pl.BlockSpec(memory_space=pltpu.SMEM)
PARAMS = pltpu.CompilerParams(vmem_limit_bytes=48 * 1024 * 1024)


def by_rows(left, right):
    return lax.dot_general(
        left, right, (((1,), (1,)), ((), ())), preferred_element_type=jnp.float32
    )


def call(body, shapes, operands, scratch=()):
    return pl.pallas_call(
        body,
        out_shape=shapes,
        in_specs=[SMEM if item.dtype == jnp.int32 else VMEM for item in operands],
        out_specs=jax.tree.map(lambda _: VMEM, shapes),
        scratch_shapes=scratch,
        compiler_params=PARAMS,
    )(*operands)


def partial_body(order_ref, series_ref, reduction_ref, *out_refs):
    rows = out_refs[0].shape[0]
    for place, out_ref in enumerate(out_refs):
        picked = pl.ds(pl.multiple_of(order_ref[place] * rows, rows), rows)
        out_ref[...] = jnp.dot(
            series_ref[picked, :], reduction_ref[...], preferred_element_type=jnp.float32
        )


def partial_sums(order, series, reduction, rows):
    shape = jax.ShapeDtypeStruct((rows, reduction.shape[1]), jnp.float32)
    return call(partial_body, (shape,) * order.shape[0], (order, series, reduction))


def eye_of(shape):
    return (
        lax.broadcasted_iota(jnp.int32, shape, 0) == lax.broadcasted_iota(jnp.int32, shape, 1)
    ).astype(jnp.float32)


def moment_of(groups, weights):
    parts = []
    for rows in groups:
        activity = by_rows(weights, rows)
        parts.append(by_rows(jnp.tanh(activity).astype(jnp.bfloat16), activity.astype(jnp.bfloat16)))
    return (parts[0] + parts[3]) + (parts[1] + parts[2])


def groups_of(refs, places):
    rows = refs[0].shape[0]
    found = [[], [], [], []]
    for k in range(places):
        own, first, second = refs[3 * k : 3 * k + 3]
        found[0].append(own[...])
        found[1].append(first[...])
        found[2].append(second[0])
        found[3].append(second[1])
    return [jnp.concatenate(group, axis=0) if places > 1 else group[0] for group in found]


def share_of(moment, gray_total):
    return 0.5 * eye_of(moment.shape) - moment / gray_total


def stepped(own_ref, other_ref, weights_ref):
    gradient = own_ref[...].astype(jnp.float32) + other_ref[...].astype(jnp.float32)
    comps = gradient.shape[0]
    size = jnp.sqrt(jnp.sum(gradient * gradient))
    rate = 0.25 * jnp.sqrt(jnp.float32(comps)) / jnp.maximum(size, 1.0)
    weights = weights_ref[...].astype(jnp.float32)
    product = jnp.dot(
        gradient.astype(jnp.bfloat16), weights.astype(jnp.bfloat16), preferred_element_type=jnp.float32
    )
    return weights + rate * product


def round_body(places, gray_total, update, carried, last, *refs):
    refs = list(refs)
    if update:
        own_ref, other_ref = refs.pop(0), refs.pop(0)
    weights_ref = refs.pop(0)
    total_ref = refs.pop(0) if carried else None
    if update:
        weights = stepped(own_ref, other_ref, weights_ref)
        refs[-2][...] = weights
    else:
        weights = weights_ref[...]
    moment = moment_of(groups_of(refs, places), weights.astype(jnp.bfloat16))
    if carried:
        moment = moment + total_ref[...]
    refs[-1][...] = share_of(moment, gray_total).astype(jnp.bfloat16) if last else moment


def last_body(place_ref, own_ref, other_ref, weights_ref, reduced_ref, unmixing_ref, sources_ref, rows_ref, held_ref):
    weights = stepped(own_ref, other_ref, weights_ref)
    held_ref[...] = weights
    sources_ref[...] = by_rows(reduced_ref[...], weights.astype(jnp.bfloat16)).astype(jnp.bfloat16)
    rows = rows_ref.shape[0]
    start = unmixing_ref[...]
    rows_ref[...] = held_ref[pl.ds(pl.multiple_of(place_ref[0] * rows, rows), rows), :] + (
        start - start.astype(jnp.bfloat16).astype(jnp.float32)
    )


def shards(narrow_count, wide_count, series, reduction, unmixing):
    narrow, wide = lax.axis_index("narrow"), lax.axis_index("wide")
    core = narrow % 2
    comps = reduction.shape[1]
    rows = series.shape[0] // narrow_count
    gray_total = series.shape[0] * wide_count

    def over(value, partner):
        pairs = []
        for n in range(narrow_count):
            for w in range(wide_count):
                to = partner(n, w)
                pairs.append((n * wide_count + w, to[0] * wide_count + to[1]))
        return lax.ppermute(value, AXES, pairs)

    def core_swap(value):
        return over(value, lambda n, w: (n ^ 1, w))

    def x_swap(value):
        return over(value, lambda n, w: (n ^ 2, w))

    def line_swap(value, k):
        return over(value, lambda n, w: (n, w ^ (2 * k)))

    def plane_one(value):
        return over(value, lambda n, w: (n, w ^ 1) if n % 2 else (n ^ 2, w))

    def plane_two(value):
        return over(value, lambda n, w: (n ^ 2, w) if n % 2 else (n, w ^ 1))

    own_rows = unmixing.shape[0]
    half = own_rows // 2
    mine = lax.dynamic_slice_in_dim(unmixing, core * half, half, 0).astype(jnp.bfloat16)
    gathered = lax.all_to_all(
        jnp.broadcast_to(mine[None], (wide_count, half, comps)), "wide", 0, 0
    )
    others = core_swap(gathered)
    low, high = jnp.where(core == 0, gathered, others), jnp.where(core == 0, others, gathered)
    weights = jnp.stack([low, high], axis=1).reshape(comps, comps)

    order = jnp.stack([narrow ^ 3, narrow ^ 1, narrow ^ 2, narrow]).astype(jnp.int32)
    send_far, send_near, keep_far, keep_near = partial_sums(order, series, reduction, rows)
    far = (keep_far + core_swap(send_far)).astype(jnp.bfloat16)
    near = keep_near + core_swap(send_near)
    own = (near + x_swap(far).astype(jnp.float32)).astype(jnp.bfloat16)

    line = wide_count // 2
    blocks = [own] + [line_swap(own, k) for k in sorted(range(1, line), key=lambda k: (k ^ (k >> 1)) & 1 or 2)]
    gathered_rows = []
    for block in blocks:
        first = plane_one(block)
        second = plane_two(jnp.stack([block, first]))
        gathered_rows += [block, first, second]

    square16 = jax.ShapeDtypeStruct((comps, comps), jnp.bfloat16)
    square32 = jax.ShapeDtypeStruct((comps, comps), jnp.float32)
    at_once = max(1, CHUNK_BYTES // (3 * blocks[0].size * blocks[0].dtype.itemsize))
    starts = range(0, len(blocks), at_once)
    shared = None
    for _ in range(ITERS):
        total = None
        for begin in starts:
            chunk = gathered_rows[3 * begin : 3 * (begin + at_once)]
            update, last = shared is not None and begin == 0, begin == starts[-1]
            operands = [shared, core_swap(shared)] if update else []
            operands += [weights] if total is None else [weights, total]
            result = square16 if last else square32
            out = call(
                functools.partial(round_body, len(chunk) // 3, gray_total, update, total is not None, last),
                (square32, result) if update else (result,),
                (*operands, *chunk),
            )
            total = out[-1]
            weights = out[0] if update else weights
        shared = total
    return call(
        last_body,
        (
            jax.ShapeDtypeStruct((rows, comps), jnp.bfloat16),
            jax.ShapeDtypeStruct((own_rows, comps), jnp.float32),
        ),
        (wide[None].astype(jnp.int32), shared, core_swap(shared), weights, own, unmixing),
        (pltpu.VMEM((comps, comps), jnp.float32),),
    )


def solution(mesh):
    return jax.shard_map(
        functools.partial(shards, mesh.shape["narrow"], mesh.shape["wide"]),
        mesh=mesh,
        in_specs=(P("wide", "narrow"), P("narrow", None), P("wide", None)),
        out_specs=(P(("wide", "narrow"), None), P("wide", None)),
        check_vma=False,
    )
```

```python
import functools

import jax
import jax.numpy as jnp
from jax import lax
from jax.experimental import pallas as pl
from jax.experimental.pallas import tpu as pltpu
from jax.sharding import PartitionSpec as P

ITERS = 2
AXES = ("narrow", "wide")
MIB = 1024 * 1024
CHUNK_BYTES = 4 * MIB
VMEM = pl.BlockSpec(memory_space=pltpu.VMEM)
SMEM = pl.BlockSpec(memory_space=pltpu.SMEM)
ANY = pl.BlockSpec(memory_space=pl.ANY)

AFTER = {
    "z3": ("wz1",),
    "z2": ("wz3",),
    "p3": ("p0",),
    "p2": ("p1",),
    "wy": ("p0",),
    "wc": ("p1",),
}


def after(value, *earlier):
    return lax.optimization_barrier((value, *earlier))[0] if earlier else value


def by_rows(left, right):
    return lax.dot_general(
        left, right, (((1,), (1,)), ((), ())), preferred_element_type=jnp.float32
    )


def call(body, shapes, operands, specs=None, scratch=(), limit=24 * MIB):
    return pl.pallas_call(
        body,
        out_shape=shapes,
        in_specs=specs or [SMEM if item.dtype == jnp.int32 else VMEM for item in operands],
        out_specs=jax.tree.map(lambda _: VMEM, shapes),
        scratch_shapes=scratch,
        compiler_params=pltpu.CompilerParams(vmem_limit_bytes=limit),
    )(*operands)


def partial_body(order_ref, series_ref, reduction_ref, *refs):
    out_refs, (left_ref, right_ref, sem_ref) = refs[:-3], refs[-3:]
    copies = [
        pltpu.make_async_copy(reduction_ref, right_ref, sem_ref.at[0]),
        pltpu.make_async_copy(series_ref, left_ref, sem_ref.at[1]),
    ]
    for copy in copies:
        copy.start()
    for copy in copies:
        copy.wait()
    rows = out_refs[0].shape[0]
    for place, out_ref in enumerate(out_refs):
        picked = pl.ds(pl.multiple_of(order_ref[place] * rows, rows), rows)
        out_ref[...] = jnp.dot(left_ref[picked, :], right_ref[...], preferred_element_type=jnp.float32)


def partial_sums(order, series, reduction, rows):
    shape = jax.ShapeDtypeStruct((rows, reduction.shape[1]), jnp.float32)
    return call(
        partial_body,
        (shape,) * order.shape[0],
        (order, series, reduction),
        specs=[SMEM, ANY, ANY],
        scratch=(
            pltpu.VMEM(series.shape, series.dtype),
            pltpu.VMEM(reduction.shape, reduction.dtype),
            pltpu.SemaphoreType.DMA((2,)),
        ),
        limit=52 * MIB + 7 * MIB // 10,
    )


def place_body(places_ref, mine_ref, other_ref, out_ref):
    rows = mine_ref.shape[-2]
    pieces = [ref[j, k] for ref in (mine_ref, other_ref) for j in range(ref.shape[0]) for k in range(ref.shape[1])]
    for n, piece in enumerate(pieces):
        out_ref[pl.ds(pl.multiple_of(places_ref[n] * rows, rows), rows), :] = piece


def joined(parts):
    return jnp.concatenate(parts, axis=0) if len(parts) > 1 else parts[0]


def moment_of(flag, refs, weights):
    owns, firsts = [ref[...] for ref in refs[0::3]], [ref[...] for ref in refs[1::3]]
    sides, across = [ref[0] for ref in refs[2::3]], [ref[1] for ref in refs[2::3]]
    lower = [jnp.where(flag, first, side) for first, side in zip(firsts, sides)]
    upper = [jnp.where(flag, side, first) for first, side in zip(firsts, sides)]
    moments = []
    for rows in (joined(owns + across), joined(lower + upper)):
        activity = by_rows(weights, rows)
        moments.append(by_rows(jnp.tanh(activity).astype(jnp.bfloat16), activity.astype(jnp.bfloat16)))
    return moments[0] + moments[1]


def stepped(own_ref, other_ref, weights_ref):
    gradient = own_ref[...].astype(jnp.float32) + other_ref[...].astype(jnp.float32)
    size = jnp.sqrt(jnp.sum(gradient * gradient))
    rate = 0.25 * jnp.sqrt(jnp.float32(gradient.shape[0])) / jnp.maximum(size, 1.0)
    weights = weights_ref[...].astype(jnp.float32)
    product = jnp.dot(
        gradient.astype(jnp.bfloat16), weights.astype(jnp.bfloat16), preferred_element_type=jnp.float32
    )
    return weights + rate * product


def round_body(gray_total, update, carried, last, core_ref, *refs):
    refs = list(refs)
    step_refs = [refs.pop(0) for _ in range(2)] if update else []
    weights_ref = refs.pop(0)
    total_ref = refs.pop(0) if carried else None
    out_ref = refs.pop()
    if update:
        weights = stepped(*step_refs, weights_ref)
        refs.pop()[...] = weights
    else:
        weights = weights_ref[...]
    total = moment_of(core_ref[0] == 0, refs, weights.astype(jnp.bfloat16))
    if carried:
        total = total + total_ref[...]
    if last:
        places = [lax.broadcasted_iota(jnp.int32, total.shape, axis) for axis in (0, 1)]
        total = (0.5 * (places[0] == places[1]).astype(jnp.float32) - total / gray_total).astype(jnp.bfloat16)
    out_ref[...] = total


def last_body(rounded, place_ref, own_ref, other_ref, weights_ref, reduced_ref, start_ref, sources_ref, rows_ref, held_ref):
    weights = stepped(own_ref, other_ref, weights_ref)
    held_ref[...] = weights
    sources_ref[...] = by_rows(reduced_ref[...], weights.astype(jnp.bfloat16)).astype(jnp.bfloat16)
    rows = rows_ref.shape[0]
    found = held_ref[pl.ds(pl.multiple_of(place_ref[0] * rows, rows), rows), :]
    if rounded:
        start = start_ref[...]
        found = found + (start - start.astype(jnp.bfloat16).astype(jnp.float32))
    rows_ref[...] = found


def shards(narrow_count, wide_count, series, reduction, unmixing):
    narrow, wide = lax.axis_index("narrow"), lax.axis_index("wide")
    core = narrow % 2
    comps, own_rows = reduction.shape[1], unmixing.shape[0]
    rows, half = series.shape[0] // narrow_count, own_rows // 2
    gray_total = series.shape[0] * wide_count
    offsets = sorted(range(1, wide_count // 2), key=lambda k: (k < 2, -k))
    riding = half % 16 == 0
    done = {}

    def permute(name, value, partner):
        pairs = []
        for n in range(narrow_count):
            for w in range(wide_count):
                there = partner(n, w)
                pairs.append((n * wide_count + w, there[0] * wide_count + there[1]))
        value = after(value, *(done[earlier] for earlier in AFTER.get(name, ()) if earlier in done))
        done[name] = lax.ppermute(value, AXES, pairs)
        return done[name]

    def core_swap(name, value):
        return permute(name, value, lambda n, w: (n ^ 1, w))

    def line_swap(name, value, k):
        return permute(name, value, lambda n, w: (n, w ^ (2 * k)))

    def plane_one(name, value):
        return permute(name, value, lambda n, w: (n, w ^ 1) if n % 2 else (n ^ 2, w))

    def plane_two(name, value):
        return permute(name, value, lambda n, w: (n ^ 2, w) if n % 2 else (n, w ^ 1))

    order = jnp.stack([narrow ^ 3, narrow ^ 1, narrow ^ 2, narrow]).astype(jnp.int32)
    send_far, send_near, keep_far, keep_near = partial_sums(order, series, reduction, rows)
    far = (keep_far + core_swap("cf", send_far)).astype(jnp.bfloat16)
    near = keep_near + core_swap("cn", send_near)
    arrived = permute("x", far, lambda n, w: (n ^ 2, w))
    own = (near + arrived.astype(jnp.float32)).astype(jnp.bfloat16)

    blocks = {0: own}

    def over_line(k):
        blocks[k] = line_swap(f"z{k}", own, k)

    def over_plane(k):
        first = plane_one(f"p{k}", blocks[k])
        return lambda: (blocks[k], first, plane_two(f"q{k}", jnp.stack([blocks[k], first])))

    mine = lax.dynamic_slice_in_dim(unmixing, core * half, half, 0).astype(jnp.bfloat16)
    if riding:
        along = jnp.stack([mine] + [line_swap(f"wz{k}", mine, k) for k in offsets])
    finish = {0: over_plane(0)}
    for k in offsets:
        over_line(k)
    gathered = {0: finish[0]()}
    if riding:
        paired = jnp.stack([along, permute("wy", along, lambda n, w: (n, w ^ 1))])
    early, late = [k for k in offsets if k != 2], [k for k in offsets if k == 2]
    for k in early:
        finish[k] = over_plane(k)
    if riding:
        swapped = core_swap("wc", paired)
        places = [
            (wide ^ (2 * k + j)) * 2 + by for by in (core, 1 - core) for j in range(2) for k in [0] + offsets
        ]
        weights = call(
            place_body,
            jax.ShapeDtypeStruct((comps, comps), jnp.bfloat16),
            (jnp.stack(places).astype(jnp.int32), paired, swapped),
        )
    else:
        weights = lax.all_gather(unmixing, "wide", axis=0, tiled=True)
    for k in early:
        gathered[k] = finish[k]()
    for k in late:
        gathered[k] = over_plane(k)()

    at_once = max(1, CHUNK_BYTES // (4 * own.size * own.dtype.itemsize))

    def cut(names):
        return [names[begin : begin + at_once] for begin in range(0, len(names), at_once)]

    shared = None
    core = core[None].astype(jnp.int32)
    for _ in range(ITERS):
        total = None
        chunks = cut([0] + offsets) if shared is not None else cut([0] + early) + cut(late)
        for number, chunk in enumerate(chunks):
            update, last = shared is not None and number == 0, number == len(chunks) - 1
            operands = [shared, core_swap("m", shared)] if update else []
            operands += [weights] if total is None else [weights, total]
            square = jax.ShapeDtypeStruct((comps, comps), jnp.float32)
            result = jax.ShapeDtypeStruct((comps, comps), jnp.bfloat16) if last else square
            out = call(
                functools.partial(round_body, gray_total, update, total is not None, last),
                (square, result) if update else (result,),
                (core, *operands, *(part for k in chunk for part in gathered[k])),
            )
            total = out[-1]
            weights = out[0] if update else weights
        shared = total
    return call(
        functools.partial(last_body, riding),
        (
            jax.ShapeDtypeStruct((rows, comps), jnp.bfloat16),
            jax.ShapeDtypeStruct((own_rows, comps), jnp.float32),
        ),
        (wide[None].astype(jnp.int32), shared, core_swap("m", shared), weights, own, unmixing),
        scratch=(pltpu.VMEM((comps, comps), jnp.float32),),
    )


def solution(mesh):
    return jax.shard_map(
        functools.partial(shards, mesh.shape["narrow"], mesh.shape["wide"]),
        mesh=mesh,
        in_specs=(P("wide", "narrow"), P("narrow", None), P("wide", None)),
        out_specs=(P(("wide", "narrow"), None), P("wide", None)),
        check_vma=False,
    )
```

```python
import functools

import jax
import jax.numpy as jnp
from jax import lax
from jax.experimental import pallas as pl
from jax.experimental.pallas import tpu as pltpu
from jax.sharding import PartitionSpec as P

ITERS = 2
AXES = ("narrow", "wide")
MIB = 1024 * 1024
CHUNK_BYTES = 4 * MIB
VMEM = pl.BlockSpec(memory_space=pltpu.VMEM)
SMEM = pl.BlockSpec(memory_space=pltpu.SMEM)
ANY = pl.BlockSpec(memory_space=pl.ANY)

ORDER = ("cf", "cn", "x", "w2", "p0", "z3", "z2", "z1", "w1", "q0", "wy", "p3", "p1", "wc", "q1", "q3", "p2", "q2")
AFTER = {"wy": ("p0",), "p2": ("q0", "p1"), "q2": ("q1", "wc")}


def after(value, *earlier):
    return lax.optimization_barrier((value, *earlier))[0] if earlier else value


def by_rows(left, right):
    return lax.dot_general(
        left, right, (((1,), (1,)), ((), ())), preferred_element_type=jnp.float32
    )


def call(body, shapes, operands, specs=None, scratch=(), limit=24 * MIB):
    return pl.pallas_call(
        body,
        out_shape=shapes,
        in_specs=specs or [SMEM if item.dtype == jnp.int32 else VMEM for item in operands],
        out_specs=jax.tree.map(lambda _: VMEM, shapes),
        scratch_shapes=scratch,
        compiler_params=pltpu.CompilerParams(vmem_limit_bytes=limit),
    )(*operands)


def partial_body(order_ref, series_ref, reduction_ref, *refs):
    out_refs, (left_ref, right_ref, sem_ref) = refs[:-3], refs[-3:]
    copies = [
        pltpu.make_async_copy(reduction_ref, right_ref, sem_ref.at[0]),
        pltpu.make_async_copy(series_ref, left_ref, sem_ref.at[1]),
    ]
    for copy in copies:
        copy.start()
    for copy in copies:
        copy.wait()
    rows = out_refs[0].shape[0]
    for place, out_ref in enumerate(out_refs):
        picked = pl.ds(pl.multiple_of(order_ref[place] * rows, rows), rows)
        out_ref[...] = jnp.dot(left_ref[picked, :], right_ref[...], preferred_element_type=jnp.float32)


def partial_sums(order, series, reduction, rows):
    shape = jax.ShapeDtypeStruct((rows, reduction.shape[1]), jnp.float32)
    return call(
        partial_body,
        (shape,) * order.shape[0],
        (order, series, reduction),
        specs=[SMEM, ANY, ANY],
        scratch=(
            pltpu.VMEM(series.shape, series.dtype),
            pltpu.VMEM(reduction.shape, reduction.dtype),
            pltpu.SemaphoreType.DMA((2,)),
        ),
        limit=52 * MIB + 7 * MIB // 10,
    )


def place_body(places_ref, mine_ref, other_ref, out_ref):
    rows, pieces = out_ref.shape[0] // places_ref.shape[0], places_ref.shape[0] // 2
    for n in range(2 * pieces):
        ref = mine_ref if n < pieces else other_ref
        piece = ref[n % pieces * rows : (n % pieces + 1) * rows, :]
        out_ref[pl.ds(pl.multiple_of(places_ref[n] * rows, rows), rows), :] = piece


def joined(parts):
    return jnp.concatenate(parts, axis=0) if len(parts) > 1 else parts[0]


def moment_of(flag, refs, weights):
    owns, firsts = [ref[...] for ref in refs[0::3]], [ref[...] for ref in refs[1::3]]
    sides, across = [ref[0] for ref in refs[2::3]], [ref[1] for ref in refs[2::3]]
    lower = [jnp.where(flag, first, side) for first, side in zip(firsts, sides)]
    upper = [jnp.where(flag, side, first) for first, side in zip(firsts, sides)]
    moments = []
    for rows in (joined(owns + across), joined(lower + upper)):
        activity = by_rows(weights, rows)
        moments.append(by_rows(jnp.tanh(activity).astype(jnp.bfloat16), activity.astype(jnp.bfloat16)))
    return moments[0] + moments[1]


def stepped(own_ref, other_ref, weights_ref):
    gradient = own_ref[...].astype(jnp.float32) + other_ref[...].astype(jnp.float32)
    size = jnp.sqrt(jnp.sum(gradient * gradient))
    rate = 0.25 * jnp.sqrt(jnp.float32(gradient.shape[0])) / jnp.maximum(size, 1.0)
    weights = weights_ref[...].astype(jnp.float32)
    product = jnp.dot(
        gradient.astype(jnp.bfloat16), weights.astype(jnp.bfloat16), preferred_element_type=jnp.float32
    )
    return weights + rate * product


def round_body(gray_total, update, carried, last, core_ref, *refs):
    refs = list(refs)
    step_refs = [refs.pop(0) for _ in range(2)] if update else []
    weights_ref = refs.pop(0)
    total_ref = refs.pop(0) if carried else None
    out_ref = refs.pop()
    if update:
        weights = stepped(*step_refs, weights_ref)
        refs.pop()[...] = weights
    else:
        weights = weights_ref[...]
    total = moment_of(core_ref[0] == 0, refs, weights.astype(jnp.bfloat16))
    if carried:
        total = total + total_ref[...]
    if last:
        places = [lax.broadcasted_iota(jnp.int32, total.shape, axis) for axis in (0, 1)]
        total = (0.5 * (places[0] == places[1]).astype(jnp.float32) - total / gray_total).astype(jnp.bfloat16)
    out_ref[...] = total


def last_body(rounded, place_ref, own_ref, other_ref, weights_ref, reduced_ref, start_ref, sources_ref, rows_ref, held_ref):
    weights = stepped(own_ref, other_ref, weights_ref)
    held_ref[...] = weights
    sources_ref[...] = by_rows(reduced_ref[...], weights.astype(jnp.bfloat16)).astype(jnp.bfloat16)
    rows = rows_ref.shape[0]
    found = held_ref[pl.ds(pl.multiple_of(place_ref[0] * rows, rows), rows), :]
    if rounded:
        start = start_ref[...]
        found = found + (start - start.astype(jnp.bfloat16).astype(jnp.float32))
    rows_ref[...] = found


def shards(narrow_count, wide_count, series, reduction, unmixing):
    narrow, wide = lax.axis_index("narrow"), lax.axis_index("wide")
    core = narrow % 2
    comps, own_rows = reduction.shape[1], unmixing.shape[0]
    rows, half = series.shape[0] // narrow_count, own_rows // 2
    gray_total = series.shape[0] * wide_count
    line = wide_count // 2
    offsets = sorted(range(1, line), key=lambda k: (k == 2, k < 2, -k))
    bits = [line >> (n + 1) for n in range(line.bit_length() - 1)]
    riding = half % 16 == 0
    done, held = {}, {}

    def permute(name, value, partner):
        pairs = []
        for n in range(narrow_count):
            for w in range(wide_count):
                there = partner(n, w)
                pairs.append((n * wide_count + w, there[0] * wide_count + there[1]))
        value = after(value, *(done[earlier] for earlier in AFTER.get(name, ()) if earlier in done))
        done[name] = lax.ppermute(value, AXES, pairs)
        return done[name]

    def core_swap(name, value):
        return permute(name, value, lambda n, w: (n ^ 1, w))

    def line_swap(name, value, k):
        return permute(name, value, lambda n, w: (n, w ^ (2 * k)))

    def plane_one(name, value):
        return permute(name, value, lambda n, w: (n, w ^ 1) if n % 2 else (n ^ 2, w))

    def plane_two(name, value):
        return permute(name, value, lambda n, w: (n ^ 2, w) if n % 2 else (n, w ^ 1))

    order = jnp.stack([narrow ^ 3, narrow ^ 1, narrow ^ 2, narrow]).astype(jnp.int32)
    send_far, send_near, keep_far, keep_near = partial_sums(order, series, reduction, rows)
    held["w"] = lax.dynamic_slice_in_dim(unmixing, core * half, half, 0).astype(jnp.bfloat16)

    def do(name):
        kind, k = name[0], int("0" + name[1:]) if name[1:].isdigit() else 0
        if name == "cf":
            held["far"] = (keep_far + core_swap(name, send_far)).astype(jnp.bfloat16)
        elif name == "cn":
            held["near"] = keep_near + core_swap(name, send_near)
        elif name == "x":
            arrived = permute(name, held["far"], lambda n, w: (n ^ 2, w))
            held["z0"] = (held["near"] + arrived.astype(jnp.float32)).astype(jnp.bfloat16)
        elif name == "wc":
            held[name] = core_swap(name, held["w"])
        elif name == "wy":
            held["w"] = jnp.concatenate([held["w"], permute(name, held["w"], lambda n, w: (n, w ^ 1))], axis=0)
        elif kind == "w":
            held["w"] = jnp.concatenate([held["w"], line_swap(name, held["w"], k)], axis=0)
        elif kind == "z":
            held[name] = line_swap(name, held["z0"], k)
        elif kind == "p":
            held[name] = plane_one(name, held[f"z{k}"])
        else:
            held[name] = plane_two(name, jnp.stack([held[f"z{k}"], held[f"p{k}"]]))

    if line == 4:
        names = ORDER
    else:
        names = ["cf", "cn", "x", *(f"w{k}" for k in bits), "wy", "wc", *(f"z{k}" for k in offsets)]
        names += [f"{kind}{k}" for k in [0] + offsets for kind in "pq"]
    for name in names:
        if riding or name[0] != "w":
            do(name)
    own = held["z0"]
    gathered = {k: [held[f"z{k}"], held[f"p{k}"], held[f"q{k}"]] for k in [0] + offsets}
    if riding:
        origins = [0]
        for bit in bits:
            origins = origins + [k ^ bit for k in origins]
        places = [(wide ^ (2 * k + j)) * 2 + by for by in (core, 1 - core) for j in range(2) for k in origins]
        weights = call(
            place_body,
            jax.ShapeDtypeStruct((comps, comps), jnp.bfloat16),
            (jnp.stack(places).astype(jnp.int32), held["w"], held["wc"]),
        )
    else:
        weights = lax.all_gather(unmixing, "wide", axis=0, tiled=True)
    at_once = max(1, CHUNK_BYTES // (4 * own.size * own.dtype.itemsize))

    def cut(names):
        return [names[begin : begin + at_once] for begin in range(0, len(names), at_once)]

    shared = None
    core = core[None].astype(jnp.int32)
    for _ in range(ITERS):
        total = None
        chunks = cut([0] + offsets) if shared is not None else cut([0] + offsets[:-1]) + [offsets[-1:]]
        for number, chunk in enumerate(chunks):
            update, last = shared is not None and number == 0, number == len(chunks) - 1
            operands = [shared, core_swap("m", shared)] if update else []
            operands += [weights] if total is None else [weights, total]
            square = jax.ShapeDtypeStruct((comps, comps), jnp.float32)
            result = jax.ShapeDtypeStruct((comps, comps), jnp.bfloat16) if last else square
            out = call(
                functools.partial(round_body, gray_total, update, total is not None, last),
                (square, result) if update else (result,),
                (core, *operands, *(part for k in chunk for part in gathered[k])),
            )
            total = out[-1]
            weights = out[0] if update else weights
        shared = total
    return call(
        functools.partial(last_body, riding),
        (
            jax.ShapeDtypeStruct((rows, comps), jnp.bfloat16),
            jax.ShapeDtypeStruct((own_rows, comps), jnp.float32),
        ),
        (wide[None].astype(jnp.int32), shared, core_swap("m", shared), weights, own, unmixing),
        scratch=(pltpu.VMEM((comps, comps), jnp.float32),),
    )


def solution(mesh):
    return jax.shard_map(
        functools.partial(shards, mesh.shape["narrow"], mesh.shape["wide"]),
        mesh=mesh,
        in_specs=(P("wide", "narrow"), P("narrow", None), P("wide", None)),
        out_specs=(P(("wide", "narrow"), None), P("wide", None)),
        check_vma=False,
    )
```

```python
import functools

import jax
import jax.numpy as jnp
from jax import lax
from jax.experimental import pallas as pl
from jax.experimental.pallas import tpu as pltpu
from jax.sharding import PartitionSpec as P

ITERS = 2
AXES = ("narrow", "wide")
MIB = 1024 * 1024
CHUNK_BYTES = 4 * MIB
VMEM = pl.BlockSpec(memory_space=pltpu.VMEM)
SMEM = pl.BlockSpec(memory_space=pltpu.SMEM)
ANY = pl.BlockSpec(memory_space=pl.ANY)

ORDER = ("cf", "cn", "x", "w2", "p0", "z3", "z2", "z1", "w1", "q0", "wy", "p3", "p1", "q3", "q1", "p2", "wc", "q2")
AFTER = {"w1": ("z1",), "wy": ("z3",), "p2": ("q0", "p1"), "wc": ("p2",), "q2": ("q1",)}


def after(value, *earlier):
    return lax.optimization_barrier((value, *earlier))[0] if earlier else value


def by_rows(left, right):
    return lax.dot_general(
        left, right, (((1,), (1,)), ((), ())), preferred_element_type=jnp.float32
    )


def call(body, shapes, operands, specs=None, scratch=(), limit=24 * MIB):
    return pl.pallas_call(
        body,
        out_shape=shapes,
        in_specs=specs or [SMEM if item.dtype == jnp.int32 else VMEM for item in operands],
        out_specs=jax.tree.map(lambda _: VMEM, shapes),
        scratch_shapes=scratch,
        compiler_params=pltpu.CompilerParams(vmem_limit_bytes=limit),
    )(*operands)


def partial_body(order_ref, series_ref, reduction_ref, *refs):
    out_refs, (left_ref, right_ref, sem_ref) = refs[:-3], refs[-3:]
    copies = [
        pltpu.make_async_copy(reduction_ref, right_ref, sem_ref.at[0]),
        pltpu.make_async_copy(series_ref, left_ref, sem_ref.at[1]),
    ]
    for copy in copies:
        copy.start()
    for copy in copies:
        copy.wait()
    rows = out_refs[0].shape[0]
    for place, out_ref in enumerate(out_refs):
        picked = pl.ds(pl.multiple_of(order_ref[place] * rows, rows), rows)
        out_ref[...] = jnp.dot(left_ref[picked, :], right_ref[...], preferred_element_type=jnp.float32)


def partial_sums(order, series, reduction, rows):
    shape = jax.ShapeDtypeStruct((rows, reduction.shape[1]), jnp.float32)
    return call(
        partial_body,
        (shape,) * order.shape[0],
        (order, series, reduction),
        specs=[SMEM, ANY, ANY],
        scratch=(
            pltpu.VMEM(series.shape, series.dtype),
            pltpu.VMEM(reduction.shape, reduction.dtype),
            pltpu.SemaphoreType.DMA((2,)),
        ),
        limit=52 * MIB + 7 * MIB // 10,
    )


def place_body(places_ref, mine_ref, other_ref, out_ref):
    rows, pieces = out_ref.shape[0] // places_ref.shape[0], places_ref.shape[0] // 2
    for n in range(2 * pieces):
        ref = mine_ref if n < pieces else other_ref
        piece = ref[n % pieces * rows : (n % pieces + 1) * rows, :]
        out_ref[pl.ds(pl.multiple_of(places_ref[n] * rows, rows), rows), :] = piece


def joined(parts):
    return jnp.concatenate(parts, axis=0) if len(parts) > 1 else parts[0]


def moment_of(flag, refs, weights):
    owns, firsts = [ref[...] for ref in refs[0::3]], [ref[...] for ref in refs[1::3]]
    sides, across = [ref[0] for ref in refs[2::3]], [ref[1] for ref in refs[2::3]]
    lower = [jnp.where(flag, first, side) for first, side in zip(firsts, sides)]
    upper = [jnp.where(flag, side, first) for first, side in zip(firsts, sides)]
    moments = []
    for rows in (joined(owns + across), joined(lower + upper)):
        activity = by_rows(weights, rows)
        moments.append(by_rows(jnp.tanh(activity).astype(jnp.bfloat16), activity.astype(jnp.bfloat16)))
    return moments[0] + moments[1]


def stepped(own_ref, other_ref, weights_ref):
    gradient = own_ref[...].astype(jnp.float32) + other_ref[...].astype(jnp.float32)
    size = jnp.sqrt(jnp.sum(gradient * gradient))
    rate = 0.25 * jnp.sqrt(jnp.float32(gradient.shape[0])) / jnp.maximum(size, 1.0)
    weights = weights_ref[...].astype(jnp.float32)
    product = jnp.dot(
        gradient.astype(jnp.bfloat16), weights.astype(jnp.bfloat16), preferred_element_type=jnp.float32
    )
    return weights + rate * product


def round_body(gray_total, update, carried, last, core_ref, *refs):
    refs = list(refs)
    step_refs = [refs.pop(0) for _ in range(2)] if update else []
    weights_ref = refs.pop(0)
    total_ref = refs.pop(0) if carried else None
    out_ref = refs.pop()
    if update:
        weights = stepped(*step_refs, weights_ref)
        refs.pop()[...] = weights
    else:
        weights = weights_ref[...]
    total = moment_of(core_ref[0] == 0, refs, weights.astype(jnp.bfloat16))
    if carried:
        total = total + total_ref[...]
    if last:
        places = [lax.broadcasted_iota(jnp.int32, total.shape, axis) for axis in (0, 1)]
        total = (0.5 * (places[0] == places[1]).astype(jnp.float32) - total / gray_total).astype(jnp.bfloat16)
    out_ref[...] = total


def last_body(rounded, place_ref, own_ref, other_ref, weights_ref, reduced_ref, start_ref, sources_ref, rows_ref, held_ref):
    weights = stepped(own_ref, other_ref, weights_ref)
    held_ref[...] = weights
    sources_ref[...] = by_rows(reduced_ref[...], weights.astype(jnp.bfloat16)).astype(jnp.bfloat16)
    rows = rows_ref.shape[0]
    found = held_ref[pl.ds(pl.multiple_of(place_ref[0] * rows, rows), rows), :]
    if rounded:
        start = start_ref[...]
        found = found + (start - start.astype(jnp.bfloat16).astype(jnp.float32))
    rows_ref[...] = found


def shards(narrow_count, wide_count, series, reduction, unmixing):
    narrow, wide = lax.axis_index("narrow"), lax.axis_index("wide")
    core = narrow % 2
    comps, own_rows = reduction.shape[1], unmixing.shape[0]
    rows, half = series.shape[0] // narrow_count, own_rows // 2
    gray_total = series.shape[0] * wide_count
    line = wide_count // 2
    offsets = sorted(range(1, line), key=lambda k: (k == 2, k < 2, -k))
    bits = [line >> (n + 1) for n in range(line.bit_length() - 1)]
    riding = half % 16 == 0
    done, held = {}, {}

    def permute(name, value, partner):
        pairs = []
        for n in range(narrow_count):
            for w in range(wide_count):
                there = partner(n, w)
                pairs.append((n * wide_count + w, there[0] * wide_count + there[1]))
        value = after(value, *(done[earlier] for earlier in AFTER.get(name, ()) if earlier in done))
        done[name] = lax.ppermute(value, AXES, pairs)
        return done[name]

    def core_swap(name, value):
        return permute(name, value, lambda n, w: (n ^ 1, w))

    def line_swap(name, value, k):
        return permute(name, value, lambda n, w: (n, w ^ (2 * k)))

    def plane_one(name, value):
        return permute(name, value, lambda n, w: (n, w ^ 1) if n % 2 else (n ^ 2, w))

    def plane_two(name, value):
        return permute(name, value, lambda n, w: (n ^ 2, w) if n % 2 else (n, w ^ 1))

    order = jnp.stack([narrow ^ 3, narrow ^ 1, narrow ^ 2, narrow]).astype(jnp.int32)
    send_far, send_near, keep_far, keep_near = partial_sums(order, series, reduction, rows)
    held["w"] = lax.dynamic_slice_in_dim(unmixing, core * half, half, 0).astype(jnp.bfloat16)

    def do(name):
        kind, k = name[0], int("0" + name[1:]) if name[1:].isdigit() else 0
        if name == "cf":
            held["far"] = (keep_far + core_swap(name, send_far)).astype(jnp.bfloat16)
        elif name == "cn":
            held["near"] = keep_near + core_swap(name, send_near)
        elif name == "x":
            arrived = permute(name, held["far"], lambda n, w: (n ^ 2, w))
            held["z0"] = (held["near"] + arrived.astype(jnp.float32)).astype(jnp.bfloat16)
        elif name == "wc":
            held[name] = core_swap(name, held["w"])
        elif name == "wy":
            held["w"] = jnp.concatenate([held["w"], permute(name, held["w"], lambda n, w: (n, w ^ 1))], axis=0)
        elif kind == "w":
            held["w"] = jnp.concatenate([held["w"], line_swap(name, held["w"], k)], axis=0)
        elif kind == "z":
            held[name] = line_swap(name, held["z0"], k)
        elif kind == "p":
            held[name] = plane_one(name, held[f"z{k}"])
        else:
            held[name] = plane_two(name, jnp.stack([held[f"z{k}"], held[f"p{k}"]]))

    if line == 4:
        names = ORDER
    else:
        names = ["cf", "cn", "x", *(f"w{k}" for k in bits), "wy", "wc", *(f"z{k}" for k in offsets)]
        names += [f"{kind}{k}" for k in [0] + offsets for kind in "pq"]
    for name in names:
        if riding or name[0] != "w":
            do(name)
    own = held["z0"]
    gathered = {k: [held[f"z{k}"], held[f"p{k}"], held[f"q{k}"]] for k in [0] + offsets}
    if riding:
        origins = [0]
        for bit in bits:
            origins = origins + [k ^ bit for k in origins]
        places = [(wide ^ (2 * k + j)) * 2 + by for by in (core, 1 - core) for j in range(2) for k in origins]
        weights = call(
            place_body,
            jax.ShapeDtypeStruct((comps, comps), jnp.bfloat16),
            (jnp.stack(places).astype(jnp.int32), held["w"], held["wc"]),
        )
    else:
        weights = lax.all_gather(unmixing, "wide", axis=0, tiled=True)
    at_once = max(1, CHUNK_BYTES // (4 * own.size * own.dtype.itemsize))

    def cut(names):
        return [names[begin : begin + at_once] for begin in range(0, len(names), at_once)]

    shared = None
    core = core[None].astype(jnp.int32)
    for _ in range(ITERS):
        total = None
        chunks = cut([0] + offsets) if shared is not None else cut([0] + offsets[:-1]) + [offsets[-1:]]
        for number, chunk in enumerate(chunks):
            update, last = shared is not None and number == 0, number == len(chunks) - 1
            operands = [shared, core_swap("m", shared)] if update else []
            operands += [weights] if total is None else [weights, total]
            square = jax.ShapeDtypeStruct((comps, comps), jnp.float32)
            result = jax.ShapeDtypeStruct((comps, comps), jnp.bfloat16) if last else square
            out = call(
                functools.partial(round_body, gray_total, update, total is not None, last),
                (square, result) if update else (result,),
                (core, *operands, *(part for k in chunk for part in gathered[k])),
            )
            total = out[-1]
            weights = out[0] if update else weights
        shared = total
    return call(
        functools.partial(last_body, riding),
        (
            jax.ShapeDtypeStruct((rows, comps), jnp.bfloat16),
            jax.ShapeDtypeStruct((own_rows, comps), jnp.float32),
        ),
        (wide[None].astype(jnp.int32), shared, core_swap("m", shared), weights, own, unmixing),
        scratch=(pltpu.VMEM((comps, comps), jnp.float32),),
    )


def solution(mesh):
    return jax.shard_map(
        functools.partial(shards, mesh.shape["narrow"], mesh.shape["wide"]),
        mesh=mesh,
        in_specs=(P("wide", "narrow"), P("narrow", None), P("wide", None)),
        out_specs=(P(("wide", "narrow"), None), P("wide", None)),
        check_vma=False,
    )
```

```python
import functools

import jax
import jax.numpy as jnp
from jax import lax
from jax.experimental import pallas as pl
from jax.experimental.pallas import tpu as pltpu
from jax.sharding import PartitionSpec as P

ITERS = 2
AXES = ("narrow", "wide")
MIB = 1024 * 1024
CHUNK_BYTES = 4 * MIB
VMEM = pl.BlockSpec(memory_space=pltpu.VMEM)
SMEM = pl.BlockSpec(memory_space=pltpu.SMEM)
ANY = pl.BlockSpec(memory_space=pl.ANY)

ORDER = ("cf", "cn", "x", "w2", "p0", "z3", "z2", "z1", "w1", "q0", "wy", "p3", "p1", "q3", "q1", "p2", "wc", "q2")
AFTER = {"w1": ("z1",), "wy": ("z3",), "q3": ("z2",), "p2": ("q0", "p1"), "wc": ("p2",), "q2": ("q1",)}


def after(value, *earlier):
    return lax.optimization_barrier((value, *earlier))[0] if earlier else value


def by_rows(left, right):
    return lax.dot_general(
        left, right, (((1,), (1,)), ((), ())), preferred_element_type=jnp.float32
    )


def call(body, shapes, operands, specs=None, scratch=(), limit=24 * MIB):
    return pl.pallas_call(
        body,
        out_shape=shapes,
        in_specs=specs or [SMEM if item.dtype == jnp.int32 else VMEM for item in operands],
        out_specs=jax.tree.map(lambda _: VMEM, shapes),
        scratch_shapes=scratch,
        compiler_params=pltpu.CompilerParams(vmem_limit_bytes=limit),
    )(*operands)


def partial_body(order_ref, series_ref, reduction_ref, *refs):
    out_refs, (left_ref, right_ref, sem_ref) = refs[:-3], refs[-3:]
    copies = [
        pltpu.make_async_copy(reduction_ref, right_ref, sem_ref.at[0]),
        pltpu.make_async_copy(series_ref, left_ref, sem_ref.at[1]),
    ]
    for copy in copies:
        copy.start()
    for copy in copies:
        copy.wait()
    rows = out_refs[0].shape[0]
    for place, out_ref in enumerate(out_refs):
        picked = pl.ds(pl.multiple_of(order_ref[place] * rows, rows), rows)
        out_ref[...] = jnp.dot(left_ref[picked, :], right_ref[...], preferred_element_type=jnp.float32)


def partial_sums(order, series, reduction, rows):
    shape = jax.ShapeDtypeStruct((rows, reduction.shape[1]), jnp.float32)
    return call(
        partial_body,
        (shape,) * order.shape[0],
        (order, series, reduction),
        specs=[SMEM, ANY, ANY],
        scratch=(
            pltpu.VMEM(series.shape, series.dtype),
            pltpu.VMEM(reduction.shape, reduction.dtype),
            pltpu.SemaphoreType.DMA((2,)),
        ),
        limit=52 * MIB + 7 * MIB // 10,
    )


def place_body(places_ref, mine_ref, other_ref, out_ref):
    rows, pieces = out_ref.shape[0] // places_ref.shape[0], places_ref.shape[0] // 2
    for n in range(2 * pieces):
        ref = mine_ref if n < pieces else other_ref
        piece = ref[n % pieces * rows : (n % pieces + 1) * rows, :]
        out_ref[pl.ds(pl.multiple_of(places_ref[n] * rows, rows), rows), :] = piece


def joined(parts):
    return jnp.concatenate(parts, axis=0) if len(parts) > 1 else parts[0]


def moment_of(flag, refs, weights):
    owns, firsts = [ref[...] for ref in refs[0::3]], [ref[...] for ref in refs[1::3]]
    sides, across = [ref[0] for ref in refs[2::3]], [ref[1] for ref in refs[2::3]]
    lower = [jnp.where(flag, first, side) for first, side in zip(firsts, sides)]
    upper = [jnp.where(flag, side, first) for first, side in zip(firsts, sides)]
    moments = []
    for rows in (joined(owns + across), joined(lower + upper)):
        activity = by_rows(weights, rows)
        moments.append(by_rows(jnp.tanh(activity).astype(jnp.bfloat16), activity.astype(jnp.bfloat16)))
    return moments[0] + moments[1]


def stepped(own_ref, other_ref, weights_ref):
    gradient = own_ref[...].astype(jnp.float32) + other_ref[...].astype(jnp.float32)
    size = jnp.sqrt(jnp.sum(gradient * gradient))
    rate = 0.25 * jnp.sqrt(jnp.float32(gradient.shape[0])) / jnp.maximum(size, 1.0)
    weights = weights_ref[...].astype(jnp.float32)
    product = jnp.dot(
        gradient.astype(jnp.bfloat16), weights.astype(jnp.bfloat16), preferred_element_type=jnp.float32
    )
    return weights + rate * product


def round_body(gray_total, update, carried, last, core_ref, *refs):
    refs = list(refs)
    step_refs = [refs.pop(0) for _ in range(2)] if update else []
    weights_ref = refs.pop(0)
    total_ref = refs.pop(0) if carried else None
    out_ref = refs.pop()
    if update:
        weights = stepped(*step_refs, weights_ref)
        refs.pop()[...] = weights
    else:
        weights = weights_ref[...]
    total = moment_of(core_ref[0] == 0, refs, weights.astype(jnp.bfloat16))
    if carried:
        total = total + total_ref[...]
    if last:
        places = [lax.broadcasted_iota(jnp.int32, total.shape, axis) for axis in (0, 1)]
        total = (0.5 * (places[0] == places[1]).astype(jnp.float32) - total / gray_total).astype(jnp.bfloat16)
    out_ref[...] = total


def last_body(rounded, place_ref, own_ref, other_ref, weights_ref, reduced_ref, start_ref, sources_ref, rows_ref, held_ref):
    weights = stepped(own_ref, other_ref, weights_ref)
    held_ref[...] = weights
    sources_ref[...] = by_rows(reduced_ref[...], weights.astype(jnp.bfloat16)).astype(jnp.bfloat16)
    rows = rows_ref.shape[0]
    found = held_ref[pl.ds(pl.multiple_of(place_ref[0] * rows, rows), rows), :]
    if rounded:
        start = start_ref[...]
        found = found + (start - start.astype(jnp.bfloat16).astype(jnp.float32))
    rows_ref[...] = found


def shards(narrow_count, wide_count, series, reduction, unmixing):
    narrow, wide = lax.axis_index("narrow"), lax.axis_index("wide")
    core = narrow % 2
    comps, own_rows = reduction.shape[1], unmixing.shape[0]
    rows, half = series.shape[0] // narrow_count, own_rows // 2
    gray_total = series.shape[0] * wide_count
    line = wide_count // 2
    offsets = sorted(range(1, line), key=lambda k: (k == 2, k < 2, -k))
    bits = [line >> (n + 1) for n in range(line.bit_length() - 1)]
    riding = half % 16 == 0
    done, held = {}, {}

    def permute(name, value, partner):
        pairs = []
        for n in range(narrow_count):
            for w in range(wide_count):
                there = partner(n, w)
                pairs.append((n * wide_count + w, there[0] * wide_count + there[1]))
        value = after(value, *(done[earlier] for earlier in AFTER.get(name, ()) if earlier in done))
        done[name] = lax.ppermute(value, AXES, pairs)
        return done[name]

    def core_swap(name, value):
        return permute(name, value, lambda n, w: (n ^ 1, w))

    def line_swap(name, value, k):
        return permute(name, value, lambda n, w: (n, w ^ (2 * k)))

    def plane_one(name, value):
        return permute(name, value, lambda n, w: (n, w ^ 1) if n % 2 else (n ^ 2, w))

    def plane_two(name, value):
        return permute(name, value, lambda n, w: (n ^ 2, w) if n % 2 else (n, w ^ 1))

    order = jnp.stack([narrow ^ 3, narrow ^ 1, narrow ^ 2, narrow]).astype(jnp.int32)
    send_far, send_near, keep_far, keep_near = partial_sums(order, series, reduction, rows)
    held["w"] = lax.dynamic_slice_in_dim(unmixing, core * half, half, 0).astype(jnp.bfloat16)

    def do(name):
        kind, k = name[0], int("0" + name[1:]) if name[1:].isdigit() else 0
        if name == "cf":
            held["far"] = (keep_far + core_swap(name, send_far)).astype(jnp.bfloat16)
        elif name == "cn":
            held["near"] = keep_near + core_swap(name, send_near)
        elif name == "x":
            arrived = permute(name, held["far"], lambda n, w: (n ^ 2, w))
            held["z0"] = (held["near"] + arrived.astype(jnp.float32)).astype(jnp.bfloat16)
        elif name == "wc":
            held[name] = core_swap(name, held["w"])
        elif name == "wy":
            held["w"] = jnp.concatenate([held["w"], permute(name, held["w"], lambda n, w: (n, w ^ 1))], axis=0)
        elif kind == "w":
            held["w"] = jnp.concatenate([held["w"], line_swap(name, held["w"], k)], axis=0)
        elif kind == "z":
            held[name] = line_swap(name, held["z0"], k)
        elif kind == "p":
            held[name] = plane_one(name, held[f"z{k}"])
        else:
            held[name] = plane_two(name, jnp.stack([held[f"z{k}"], held[f"p{k}"]]))

    if line == 4:
        names = ORDER
    else:
        names = ["cf", "cn", "x", *(f"w{k}" for k in bits), "wy", "wc", *(f"z{k}" for k in offsets)]
        names += [f"{kind}{k}" for k in [0] + offsets for kind in "pq"]
    for name in names:
        if riding or name[0] != "w":
            do(name)
    own = held["z0"]
    gathered = {k: [held[f"z{k}"], held[f"p{k}"], held[f"q{k}"]] for k in [0] + offsets}
    if riding:
        origins = [0]
        for bit in bits:
            origins = origins + [k ^ bit for k in origins]
        places = [(wide ^ (2 * k + j)) * 2 + by for by in (core, 1 - core) for j in range(2) for k in origins]
        weights = call(
            place_body,
            jax.ShapeDtypeStruct((comps, comps), jnp.bfloat16),
            (jnp.stack(places).astype(jnp.int32), held["w"], held["wc"]),
        )
    else:
        weights = lax.all_gather(unmixing, "wide", axis=0, tiled=True)
    at_once = max(1, CHUNK_BYTES // (4 * own.size * own.dtype.itemsize))

    def cut(names):
        return [names[begin : begin + at_once] for begin in range(0, len(names), at_once)]

    shared = None
    core = core[None].astype(jnp.int32)
    for _ in range(ITERS):
        total = None
        chunks = cut([0] + offsets) if shared is not None else cut([0] + offsets[:-1]) + [offsets[-1:]]
        for number, chunk in enumerate(chunks):
            update, last = shared is not None and number == 0, number == len(chunks) - 1
            operands = [shared, core_swap("m", shared)] if update else []
            operands += [weights] if total is None else [weights, total]
            square = jax.ShapeDtypeStruct((comps, comps), jnp.float32)
            result = jax.ShapeDtypeStruct((comps, comps), jnp.bfloat16) if last else square
            out = call(
                functools.partial(round_body, gray_total, update, total is not None, last),
                (square, result) if update else (result,),
                (core, *operands, *(part for k in chunk for part in gathered[k])),
            )
            total = out[-1]
            weights = out[0] if update else weights
        shared = total
    return call(
        functools.partial(last_body, riding),
        (
            jax.ShapeDtypeStruct((rows, comps), jnp.bfloat16),
            jax.ShapeDtypeStruct((own_rows, comps), jnp.float32),
        ),
        (wide[None].astype(jnp.int32), shared, core_swap("m", shared), weights, own, unmixing),
        scratch=(pltpu.VMEM((comps, comps), jnp.float32),),
    )


def solution(mesh):
    return jax.shard_map(
        functools.partial(shards, mesh.shape["narrow"], mesh.shape["wide"]),
        mesh=mesh,
        in_specs=(P("wide", "narrow"), P("narrow", None), P("wide", None)),
        out_specs=(P(("wide", "narrow"), None), P("wide", None)),
        check_vma=False,
    )
```
